32 devices in a mesh: ctx: 16 (over z, y, x), pipe: 2 (over core).
Axes of the slice: x: 2, y: 2, z: 4, core: 2. Of those that a mesh axis runs over, the one named last changes fastest.
Arguments:
- activations: float32 [2, 1, 2048, 4096], P('pipe', None, 'ctx'), may hold values from -6 to 6
- norm_gain: bfloat16 [2, 8, 4096], P('pipe', None, 'ctx'), may hold values from 0.5 to 2, as said below
- w_query: bfloat16 [2, 8, 4096, 512], P('pipe', None, 'ctx'), may hold values from -0.09375 to 0.09375
- w_keyval: bfloat16 [2, 8, 4096, 256], P('pipe', None, 'ctx'), may hold values from -0.09375 to 0.09375
- w_out: bfloat16 [2, 8, 512, 4096], P('pipe', None, None, 'ctx'), may hold values from -0.25 to 0.25
- segment_ids: int32 [1, 2048], replicated, may hold values from 0 to 3, as said below
- layer_order: int32 [2, 2], P(None, 'pipe'), may hold values from 0 to 7
Outputs:
- final_stream: float32 [2, 1, 2048, 4096], P('pipe', None, 'ctx')
The draws below stay inside these ranges and needn't reach their ends.
Inputs may be any that keep to these rules, and one draw needn't show every extreme that they name: `segment_ids`: each row never falls; every document holds 1 to 1024 positions and the last one holds exactly 1024. `norm_gain`: positive.
All inputs are finite; a program needn't handle non-finite values.
Results may differ from the reference program's by a relative error of at most 0.015.
Values may be sent and summed in bfloat16 or wider, within the bound.
A program may use at most 128 MiB of HBM per device.

```python
import math
import jax
import jax.numpy as jnp
from jax import lax

D = 4096
HEADS = 4
HD = 128
LAYERS_DEV = 8
TICKS = 2
SEQS = 1
TOK_DEV = 128
LENGTH = 2048
N_CTX = 16
N_PIPE = 2


def draw_norm_gain(key, part):
    gain_shape = (N_PIPE, LAYERS_DEV, D)
    return jnp.exp(jax.random.uniform(key, gain_shape, jnp.float32, -0.69, 0.69)).astype(jnp.bfloat16)


def draw_segment_ids(key, part):
    half = LENGTH // 2
    first_key = jax.random.fold_in(key, 11)
    second_key = jax.random.fold_in(key, 23)
    first = jax.random.randint(first_key, (SEQS, 1), 1, half - 1)
    second = first + jax.random.randint(second_key, (SEQS, 1), 1, half - first)
    places = jnp.arange(LENGTH, dtype=jnp.int32)[None, :]
    return (places >= first).astype(jnp.int32) + (places >= second).astype(jnp.int32) + (places >= half).astype(jnp.int32)


def place_ends(result, key, smallest, high):
    longest = result.shape.index(max(result.shape))
    spots = []
    for shift in (0, 1):
        where = [jax.random.randint(jax.random.fold_in(key, axis), (), 0, length) for axis, length in enumerate(result.shape)]
        where[longest] = (where[longest] + shift) % result.shape[longest]
        spots.append(tuple(where))
    return result.at[spots[0]].set(smallest).at[spots[1]].set(high)


def steps_of(rng, dims, shards, low, high):
    loudness, own = 1.0, jax.random.fold_in(rng, 6)
    for dim, parts in shards:
        draws = jnp.exp(jax.random.uniform(jax.random.fold_in(own, dim), (parts,), jnp.float32, low / len(shards), high / len(shards)))
        loudness = loudness * jnp.repeat(draws, dims[dim] // parts).reshape([-1 if axis == dim else 1 for axis in range(len(dims))])
    return loudness


def scatter_about(stream_key, shape, deviation, bound, cuts=(), kind=jnp.bfloat16):
    level = steps_of(stream_key, shape, cuts, -0.22, 0.18) if cuts else 1.0
    result = jax.random.normal(stream_key, shape, jnp.float32) * deviation * level
    return jnp.minimum(jnp.maximum(result, -bound), bound).astype(kind)


def setup_inputs(seed: int = 0) -> dict:
    splits = jax.random.split(jax.random.key(seed), 8)
    return {
        "activations": scatter_about(splits[0], (N_PIPE, SEQS, LENGTH, D), 1.0, 6.0, ((0, 2), (2, 16)), jnp.float32),
        "norm_gain": draw_norm_gain(jax.random.fold_in(splits[7], 71), 0),
        "w_query": scatter_about(splits[2], (N_PIPE, LAYERS_DEV, D, HEADS * HD), D ** -0.5, 0.09375, ((0, 2), (2, 16))),
        "w_keyval": scatter_about(splits[3], (N_PIPE, LAYERS_DEV, D, 2 * HD), D ** -0.5, 0.09375, ((0, 2), (2, 16))),
        "w_out": scatter_about(splits[4], (N_PIPE, LAYERS_DEV, HEADS * HD, D), (HEADS * HD) ** -0.5, 0.25, ((0, 2), (3, 16))),
        "segment_ids": draw_segment_ids(jax.random.fold_in(splits[7], 71), 0),
        "layer_order": place_ends(jax.random.randint(splits[6], (TICKS, N_PIPE), 0, LAYERS_DEV), jax.random.fold_in(splits[6], 1), 0, LAYERS_DEV - 1).astype(jnp.int32),
    }


def row_positions(rows):
    half = TOK_DEV // 2
    block = rows // TOK_DEV
    offset = rows % TOK_DEV
    return jnp.where(offset < half, block * half + offset, (2 * N_CTX - 1 - block) * half + offset - half).astype(jnp.int32)

def position_rows(places):
    half = TOK_DEV // 2
    block = places // half
    offset = places % half
    return jnp.where(block < N_CTX, block * TOK_DEV + offset, (2 * N_CTX - 1 - block) * TOK_DEV + half + offset).astype(jnp.int32)

def attend_sequence(query_seq, keyval_seq, segment_row):
    query_block = math.gcd(LENGTH, 1024)
    scale = 1.0 / math.sqrt(HD)
    pieces = []
    for block_index in range(LENGTH // query_block):
        first = block_index * query_block
        last = first + query_block
        query_part = query_seq[first:last].astype(jnp.float32)
        key_part = keyval_seq[:last, :HD].astype(jnp.float32)
        value_part = keyval_seq[:last, HD:].astype(jnp.float32)
        scores = jnp.einsum('qhd,kd->hqk', query_part, key_part) * scale
        query_pos = jnp.arange(first, last, dtype=jnp.int32)
        key_pos = jnp.arange(last, dtype=jnp.int32)
        allowed = (key_pos[None, :] <= query_pos[:, None]) & (segment_row[None, :last] == segment_row[first:last, None])
        scores = jnp.where(allowed[None], scores, -1e+30)
        row_max = lax.optimization_barrier(jnp.max(scores, axis=-1, keepdims=True))
        probs = jnp.where(allowed[None], jnp.exp(scores - row_max), 0.0)
        totals = lax.optimization_barrier(jnp.sum(probs, axis=-1))
        probs_low = lax.optimization_barrier(probs.astype(jnp.bfloat16))
        summed = jnp.einsum('hqk,kd->qhd', probs_low.astype(jnp.float32), value_part)
        pieces.append((summed / jnp.transpose(totals)[:, :, None]).astype(jnp.bfloat16))
    return jnp.concatenate(pieces, axis=0)

def layer_apply(stream, gain_row, query_weight, keyval_weight, out_weight, segment_ids):
    stream_f = stream.astype(jnp.float32)
    mean_square = lax.optimization_barrier(jnp.mean(stream_f * stream_f, axis=-1, keepdims=True))
    normed = (stream_f * lax.rsqrt(mean_square + 1e-05) * gain_row.astype(jnp.float32)).astype(jnp.bfloat16)
    flat = normed.reshape(SEQS * LENGTH, D)
    queries = jnp.dot(flat, query_weight, preferred_element_type=jnp.float32).astype(jnp.bfloat16)
    queries = queries.reshape(SEQS, LENGTH, HEADS, HD)
    keyvals = jnp.dot(flat, keyval_weight, preferred_element_type=jnp.float32).astype(jnp.bfloat16)
    keyvals = keyvals.reshape(SEQS, LENGTH, 2 * HD)
    places = jnp.arange(LENGTH, dtype=jnp.int32)
    by_position = position_rows(places)
    by_row = row_positions(places)
    queries = jnp.take(queries, by_position, axis=1)
    keyvals = jnp.take(keyvals, by_position, axis=1)

    def one_sequence(packed):
        query_seq, keyval_seq, segment_row = packed
        return attend_sequence(query_seq, keyval_seq, segment_row)
    attended = lax.map(one_sequence, (queries, keyvals, segment_ids))
    attended = jnp.take(attended, by_row, axis=1)
    attended = attended.reshape(SEQS * LENGTH, HEADS * HD)
    mixed = jnp.dot(attended, out_weight, preferred_element_type=jnp.float32)
    return stream_f + mixed.reshape(SEQS, LENGTH, D)

def reference(activations, norm_gain, w_query, w_keyval, w_out, segment_ids, layer_order):
    batches = [activations[index] for index in range(N_PIPE)]
    for tick_index in range(TICKS):
        for index in range(N_PIPE):
            section = (index + tick_index) % N_PIPE
            layer = layer_order[tick_index, section]
            batches[index] = layer_apply(batches[index], norm_gain[section, layer], w_query[section, layer], w_keyval[section, layer], w_out[section, layer], segment_ids)
    return jnp.stack([batches[(place - TICKS) % N_PIPE] for place in range(N_PIPE)])
```

```python
import functools
import itertools
import math

import jax
import jax.numpy as jnp
from jax import lax
from jax.experimental import pallas as pl
from jax.experimental.pallas import tpu as pltpu
from jax.sharding import PartitionSpec as P

TICKS = 2


def passed_along(array, axis, by):
    length = lax.axis_size(axis)
    return lax.ppermute(array, axis, [(i, (i + by) % length) for i in range(length)])


def grid_of(count):
    known = {16: (4, 2, 2), 32: (4, 8)}
    return known.get(count, (count,))


def orders_of(sizes):
    dims = tuple(range(len(sizes)))
    if len(dims) == 1:
        return (dims, dims)
    return (dims, dims[:-2] + (dims[-1], dims[-2]))


def gather_kernel(sizes, cuts, *refs):
    count = len(cuts)
    blocks, wholes = refs[:count], refs[count : 2 * count]
    send_sems, recv_sems, own_sems = refs[2 * count :]
    rank = len(sizes)
    strides = [math.prod(sizes[d + 1 :]) for d in range(rank)]
    me = lax.axis_index("ctx")
    coords = [(me // strides[d]) % sizes[d] for d in range(rank)]

    def place(delta):
        return sum(((coords[d] + delta[d]) % sizes[d]) * strides[d] for d in range(rank))

    def along(dim, by):
        return tuple(by if d == dim else 0 for d in range(rank))

    def flat(delta):
        return sum(delta[d] * strides[d] for d in range(rank))

    barrier = pltpu.get_barrier_semaphore()
    greeted = 0
    for dim in range(rank):
        for by in range(1, sizes[dim]):
            pl.semaphore_signal(
                barrier,
                inc=1,
                device_id={"ctx": place(along(dim, by))},
                device_id_type=pl.DeviceIdType.MESH,
            )
            greeted += 1
    pl.semaphore_wait(barrier, greeted)

    orders = orders_of(sizes)
    started = []
    used = {}

    def copy_of(which, part, delta, dim, by, send):
        rows = pl.ds(*cuts[which][part])
        source = place(delta)
        landing = wholes[which].at[source, rows]
        origin = landing if any(delta) else blocks[which].at[rows]
        seen = tuple((sizes[d] - by) % sizes[d] if d == dim else delta[d] for d in range(rank))
        return pltpu.make_async_remote_copy(
            src_ref=origin,
            dst_ref=landing,
            send_sem=send_sems.at[which, part, send],
            recv_sem=recv_sems.at[which, part, flat(seen)],
            device_id={"ctx": place(along(dim, by))},
            device_id_type=pl.DeviceIdType.MESH,
        )

    def pass_on(which, part, delta, phases):
        for phase in phases:
            dim = orders[part][phase]
            for by in range(1, sizes[dim]):
                send = used.get((which, part), 0)
                used[which, part] = send + 1
                copy = copy_of(which, part, delta, dim, by, send)
                copy.start()
                started.append(copy)

    def take(which, part, phase):
        order = orders[part]
        ranges = [range(1)] * rank
        for before in order[:phase]:
            ranges[before] = range(sizes[before])
        ranges[order[phase]] = range(1, sizes[order[phase]])
        for delta in itertools.product(*ranges):
            landing = wholes[which].at[place(delta), pl.ds(*cuts[which][part])]
            pltpu.make_async_remote_copy(
                src_ref=landing,
                dst_ref=landing,
                send_sem=send_sems.at[which, part, 0],
                recv_sem=recv_sems.at[which, part, flat(delta)],
                device_id={"ctx": place(along(order[phase], 1))},
                device_id_type=pl.DeviceIdType.MESH,
            ).wait_recv()
            pass_on(which, part, delta, range(phase + 1, rank))

    for which in range(count):
        for part in range(2):
            pass_on(which, part, (0,) * rank, range(rank))
    own = []
    for which in range(count):
        copy = pltpu.make_async_copy(blocks[which], wholes[which].at[me], own_sems.at[which])
        copy.start()
        own.append(copy)
    for turn in range(count + rank - 1):
        for which in range(count):
            phase = turn - which
            if 0 <= phase < rank:
                for part in range(2):
                    take(which, part, phase)
    for copy in own:
        copy.wait()
    for copy in started:
        copy.wait_send()


def gather_blocks(blocks, ctx_count, collective_id):
    cuts = []
    for block in blocks:
        rows = block.shape[0]
        first = rows // 32 * 16
        cuts.append(((0, first), (first, rows - first)))
    count = len(blocks)
    wholes = pl.pallas_call(
        functools.partial(gather_kernel, grid_of(ctx_count), tuple(cuts)),
        out_shape=[jax.ShapeDtypeStruct((ctx_count, *b.shape), b.dtype) for b in blocks],
        in_specs=[pl.BlockSpec(memory_space=pl.ANY)] * count,
        out_specs=[pl.BlockSpec(memory_space=pl.ANY)] * count,
        scratch_shapes=[
            pltpu.SemaphoreType.DMA((count, 2, ctx_count)),
            pltpu.SemaphoreType.DMA((count, 2, ctx_count)),
            pltpu.SemaphoreType.DMA((count,)),
        ],
        compiler_params=pltpu.CompilerParams(collective_id=collective_id, has_side_effects=True),
    )(*blocks)
    return wholes


def row_positions(rows, tok_rows, ctx_count):
    half = tok_rows // 2
    block = rows // tok_rows
    offset = rows % tok_rows
    return jnp.where(
        offset < half, block * half + offset, (2 * ctx_count - 1 - block) * half + offset - half
    )


def pick(stacked, layer):
    return lax.dynamic_index_in_dim(stacked[0], layer, 0, keepdims=False)


def attend(queries, keyvals, allowed):
    seqs_here, rows_here, head_count, head_dim = queries.shape
    keys = keyvals[..., :head_dim]
    values = keyvals[..., head_dim:]
    scores = jnp.einsum("sqhd,skd->shqk", queries, keys, preferred_element_type=jnp.float32)
    scores = scores * (1.0 / math.sqrt(head_dim))
    allowed = allowed[:, None]
    scores = jnp.where(allowed, scores, -1e30)
    top = jnp.max(scores, axis=-1, keepdims=True)
    probs = jnp.where(allowed, jnp.exp(scores - top), 0.0)
    totals = jnp.sum(probs, axis=-1)
    summed = jnp.einsum(
        "shqk,skd->sqhd", probs.astype(jnp.bfloat16), values, preferred_element_type=jnp.float32
    )
    attended = (summed / jnp.swapaxes(totals, 1, 2)[..., None]).astype(jnp.bfloat16)
    return attended.reshape(seqs_here * rows_here, head_count * head_dim)


def body(activations, norm_gain, w_query, w_keyval, w_out, segment_ids, layer_order):
    ctx_count = lax.axis_size("ctx")
    ctx_index = lax.axis_index("ctx")
    state = activations[0]
    seqs_here, tok_rows, model_width = state.shape
    query_width = w_query.shape[-1]
    kv_width = w_keyval.shape[-1]
    head_dim = kv_width // 2
    head_count = query_width // head_dim
    in_rows = w_query.shape[2]
    wide = query_width + kv_width
    in_parts, out_parts = [], []
    for tick in range(TICKS):
        layer = layer_order[tick, 0]
        gain_rows = jnp.pad(pick(norm_gain, layer)[None, :], ((0, 15), (0, wide - in_rows)))
        both = jnp.concatenate([pick(w_query, layer), pick(w_keyval, layer)], axis=1)
        in_parts.append(jnp.concatenate([both, gain_rows], axis=0))
        out_parts.append(pick(w_out, layer))
    wholes = gather_blocks(
        [part for pair in zip(in_parts, out_parts) for part in pair], ctx_count, 0
    )
    gathered = [(wholes[2 * tick], wholes[2 * tick + 1]) for tick in range(TICKS)]
    query_pos = row_positions(
        ctx_index * tok_rows + lax.iota(jnp.int32, tok_rows), tok_rows, ctx_count
    )
    query_seg = jnp.take(segment_ids, query_pos, axis=1)
    halves = segment_ids.reshape(seqs_here, 2, ctx_count, tok_rows // 2)
    by_row = jnp.stack([halves[:, 0], halves[:, 1, ::-1]], axis=2)
    key_seg = by_row.reshape(seqs_here, ctx_count * tok_rows)
    key_pos = row_positions(lax.iota(jnp.int32, ctx_count * tok_rows), tok_rows, ctx_count)
    allowed = (key_pos[None, None, :] <= query_pos[None, :, None]) & (
        key_seg[:, None, :] == query_seg[:, :, None]
    )
    for tick in range(TICKS):
        in_all, out_all = gathered[tick]
        flat = state.reshape(seqs_here * tok_rows, model_width)
        gain = in_all[:, in_rows, :in_rows].reshape(model_width)
        scaled = flat * lax.rsqrt(jnp.mean(flat * flat, axis=1, keepdims=True) + 1e-05)
        hidden = (scaled * gain.astype(jnp.float32)[None, :]).astype(jnp.bfloat16)
        sums = jnp.einsum(
            "tcd,cdw->tw",
            hidden.reshape(seqs_here * tok_rows, ctx_count, in_rows),
            in_all[:, :in_rows],
            preferred_element_type=jnp.float32,
        ).astype(jnp.bfloat16)
        queries = sums[:, :query_width].reshape(seqs_here, tok_rows, head_count, head_dim)
        (keyvals,) = gather_blocks([sums[:, query_width:]], ctx_count, 1)
        keyvals = keyvals.reshape(ctx_count, seqs_here, tok_rows, kv_width)
        keyvals = jnp.swapaxes(keyvals, 0, 1).reshape(seqs_here, ctx_count * tok_rows, kv_width)
        attended = attend(queries, keyvals, allowed)
        mixed = jnp.einsum(
            "tw,cwd->tcd", attended, out_all, preferred_element_type=jnp.float32
        ).reshape(flat.shape)
        state = (flat + mixed).reshape(seqs_here, tok_rows, model_width)
        state = passed_along(state.astype(jnp.bfloat16), "pipe", 1).astype(state.dtype)
    return state[None]


def solution(mesh):
    in_specs = (
        P("pipe", None, "ctx", None),
        P("pipe", None, "ctx"),
        P("pipe", None, "ctx", None),
        P("pipe", None, "ctx", None),
        P("pipe", None, None, "ctx"),
        P(),
        P(None, "pipe"),
    )
    out_specs = P("pipe", None, "ctx", None)
    return jax.shard_map(body, mesh=mesh, in_specs=in_specs, out_specs=out_specs, check_vma=False)
```

```python
import functools
import itertools
import math

import jax
import jax.numpy as jnp
from jax import lax
from jax.experimental import pallas as pl
from jax.experimental.pallas import tpu as pltpu
from jax.sharding import PartitionSpec as P

TICKS = 2


def passed_along(array, axis, by):
    length = lax.axis_size(axis)
    return lax.ppermute(array, axis, [(i, (i + by) % length) for i in range(length)])


def grid_of(count):
    known = {16: (4, 2, 2), 32: (4, 8)}
    return known.get(count, (count,))


def orders_of(sizes):
    dims = tuple(range(len(sizes)))
    if len(dims) == 1:
        return (dims, dims)
    return (dims, dims[:-2] + (dims[-1], dims[-2]))


def layers_kernel(sizes, cuts, *refs):
    weights = 2 * TICKS
    count = len(cuts)
    stream, bias = refs[0], refs[1]
    out = refs[2 + weights]
    scratch = refs[3 + weights :]
    blocks = refs[2 : 2 + weights] + scratch[:TICKS]
    wholes = scratch[TICKS : TICKS + count]
    queries, attended, leaving, arriving = scratch[TICKS + count : TICKS + count + 4]
    send_sems, recv_sems, own_sems, pipe_sems = scratch[TICKS + count + 4 :]
    rank = len(sizes)
    strides = [math.prod(sizes[d + 1 :]) for d in range(rank)]
    ctx_count = math.prod(sizes)
    me = lax.axis_index("ctx")
    coords = [(me // strides[d]) % sizes[d] for d in range(rank)]
    pipe_count = lax.axis_size("pipe")
    section = lax.axis_index("pipe")

    def place(delta):
        return sum(((coords[d] + delta[d]) % sizes[d]) * strides[d] for d in range(rank))

    def along(dim, by):
        return tuple(by if d == dim else 0 for d in range(rank))

    def flat(delta):
        return sum(delta[d] * strides[d] for d in range(rank))

    barrier = pltpu.get_barrier_semaphore()
    greeted = 0
    for dim in range(rank):
        for by in range(1, sizes[dim]):
            pl.semaphore_signal(
                barrier,
                inc=1,
                device_id={"ctx": place(along(dim, by))},
                device_id_type=pl.DeviceIdType.MESH,
            )
            greeted += 1
    for by in sorted({1, pipe_count - 1}):
        pl.semaphore_signal(
            barrier,
            inc=1,
            device_id={"pipe": (section + by) % pipe_count},
            device_id_type=pl.DeviceIdType.MESH,
        )
        greeted += 1
    pl.semaphore_wait(barrier, greeted)

    orders = orders_of(sizes)
    started = []
    used = {}

    def copy_of(which, part, delta, dim, by, send):
        rows = pl.ds(*cuts[which][part])
        landing = wholes[which].at[place(delta), rows]
        origin = landing if any(delta) else blocks[which].at[rows]
        seen = tuple((sizes[d] - by) % sizes[d] if d == dim else delta[d] for d in range(rank))
        return pltpu.make_async_remote_copy(
            src_ref=origin,
            dst_ref=landing,
            send_sem=send_sems.at[which, part, send],
            recv_sem=recv_sems.at[which, part, flat(seen)],
            device_id={"ctx": place(along(dim, by))},
            device_id_type=pl.DeviceIdType.MESH,
        )

    def pass_on(which, part, delta, phases):
        for phase in phases:
            dim = orders[part][phase]
            for by in range(1, sizes[dim]):
                send = used.get((which, part), 0)
                used[which, part] = send + 1
                copy = copy_of(which, part, delta, dim, by, send)
                copy.start()
                started.append(copy)

    def take(which, phase):
        for part, order in enumerate(orders):
            ranges = [range(1)] * rank
            for before in order[:phase]:
                ranges[before] = range(sizes[before])
            ranges[order[phase]] = range(1, sizes[order[phase]])
            for delta in itertools.product(*ranges):
                landing = wholes[which].at[place(delta), pl.ds(*cuts[which][part])]
                pltpu.make_async_remote_copy(
                    src_ref=landing,
                    dst_ref=landing,
                    send_sem=send_sems.at[which, part, 0],
                    recv_sem=recv_sems.at[which, part, flat(delta)],
                    device_id={"ctx": place(along(order[phase], 1))},
                    device_id_type=pl.DeviceIdType.MESH,
                ).wait_recv()
                pass_on(which, part, delta, range(phase + 1, rank))

    def own_copy(which):
        return pltpu.make_async_copy(blocks[which], wholes[which].at[me], own_sems.at[which])

    def begin(which):
        own_copy(which).start()
        for part in range(len(orders)):
            pass_on(which, part, (0,) * rank, range(rank))

    tok_rows, model_width = stream.shape
    in_rows = model_width // ctx_count
    query_width = attended.shape[1]
    head_dim = queries.shape[-1]
    head_count = query_width // head_dim
    scale = 1.0 / math.sqrt(head_dim)

    def columns(index):
        return pl.ds(pl.multiple_of(index * in_rows, in_rows), in_rows)

    def project(tick, source):
        own_copy(2 * tick).wait()
        whole = wholes[2 * tick]

        def square(index, total):
            value = source[:, columns(index)].astype(jnp.float32)
            return total + jnp.sum(value * value, axis=1, keepdims=True)

        squares = lax.fori_loop(0, ctx_count, square, jnp.zeros((tok_rows, 1), jnp.float32))
        factor = lax.rsqrt(squares / model_width + 1e-05)

        def piece(index, total):
            value = source[:, columns(index)].astype(jnp.float32)
            gain = whole[index, in_rows : in_rows + 16, :in_rows].astype(jnp.float32)[:1]
            hidden = (value * factor * gain).astype(jnp.bfloat16)
            return total + jnp.dot(
                hidden, whole[index, :in_rows, :], preferred_element_type=jnp.float32
            )

        width = whole.shape[-1]
        sums = lax.fori_loop(0, ctx_count, piece, jnp.zeros((tok_rows, width), jnp.float32))
        low = sums.astype(jnp.bfloat16)
        for head in range(head_count):
            queries[head] = low[:, head * head_dim : (head + 1) * head_dim]
        blocks[weights + tick][...] = low[:, query_width:]

    def attend(tick):
        own_copy(weights + tick).wait()
        whole = wholes[weights + tick]
        keys = whole[:, :, :head_dim].reshape(ctx_count * tok_rows, head_dim)
        values = whole[:, :, head_dim:].reshape(ctx_count * tok_rows, head_dim)
        for head in range(head_count):
            scores = lax.dot_general(
                queries[head], keys, (((1,), (1,)), ((), ())), preferred_element_type=jnp.float32
            )
            scores = scores * scale + bias[...]
            probs = jnp.exp(scores - jnp.max(scores, axis=1, keepdims=True))
            totals = jnp.sum(probs, axis=1, keepdims=True)
            summed = jnp.dot(
                probs.astype(jnp.bfloat16), values, preferred_element_type=jnp.float32
            )
            attended[:, head * head_dim : (head + 1) * head_dim] = (summed / totals).astype(
                jnp.bfloat16
            )

    def mix(tick, source, target):
        own_copy(2 * tick + 1).wait()
        whole = wholes[2 * tick + 1]

        @pl.loop(0, ctx_count)
        def _(index):
            mixed = jnp.dot(attended[...], whole[index], preferred_element_type=jnp.float32)
            value = source[:, columns(index)].astype(jnp.float32) + mixed
            target[:, columns(index)] = value.astype(jnp.bfloat16)

    last = rank - 1
    begin(0)
    begin(1)
    take(0, 0)
    begin(2)
    for phase in range(1, rank):
        take(0, phase)
        take(1, phase - 1)
    project(0, stream)
    begin(4)
    begin(3)
    for phase in range(rank):
        take(4, phase)
        if phase < last:
            take(2, phase)
    attend(0)
    for phase in range(last):
        take(3, phase)
    take(1, last)
    mix(0, stream, leaving)
    onward = pltpu.make_async_remote_copy(
        src_ref=leaving,
        dst_ref=arriving,
        send_sem=pipe_sems.at[0],
        recv_sem=pipe_sems.at[1],
        device_id={"pipe": (section + 1) % pipe_count},
        device_id_type=pl.DeviceIdType.MESH,
    )
    onward.start()
    take(2, last)
    onward.wait()
    project(1, arriving)
    begin(5)
    for phase in range(rank):
        take(5, phase)
    attend(1)
    take(3, last)
    mix(1, arriving, out)
    for copy in started:
        copy.wait_send()


def run_layers(stream, bias, blocks, ctx_count, head_dim):
    tok_rows = stream.shape[0]
    query_width = blocks[1].shape[0]
    kv_width = blocks[0].shape[1] - query_width
    shapes = [block.shape for block in blocks] + [(tok_rows, kv_width)] * TICKS
    cuts = []
    for rows, _ in shapes:
        first = rows // 32 * 16
        cuts.append(((0, first), (first, rows - first)))
    count = len(shapes)
    parts = len(cuts[0])
    low = jnp.bfloat16
    vmem = pl.BlockSpec(memory_space=pltpu.VMEM)
    return pl.pallas_call(
        functools.partial(layers_kernel, grid_of(ctx_count), tuple(cuts)),
        out_shape=jax.ShapeDtypeStruct(stream.shape, low),
        in_specs=[vmem, vmem] + [pl.BlockSpec(memory_space=pl.ANY)] * len(blocks),
        out_specs=vmem,
        scratch_shapes=[pltpu.VMEM((tok_rows, kv_width), low)] * TICKS
        + [pltpu.VMEM((ctx_count, *shape), low) for shape in shapes]
        + [
            pltpu.VMEM((query_width // head_dim, tok_rows, head_dim), low),
            pltpu.VMEM((tok_rows, query_width), low),
            pltpu.VMEM(stream.shape, low),
            pltpu.VMEM(stream.shape, low),
            pltpu.SemaphoreType.DMA((count, parts, ctx_count)),
            pltpu.SemaphoreType.DMA((count, parts, ctx_count)),
            pltpu.SemaphoreType.DMA((count,)),
            pltpu.SemaphoreType.DMA((2,)),
        ],
        compiler_params=pltpu.CompilerParams(
            collective_id=0, has_side_effects=True, vmem_limit_bytes=56 * 1024 * 1024
        ),
    )(stream, bias, *blocks)


def row_positions(rows, tok_rows, ctx_count):
    half = tok_rows // 2
    block = rows // tok_rows
    offset = rows % tok_rows
    return jnp.where(
        offset < half, block * half + offset, (2 * ctx_count - 1 - block) * half + offset - half
    )


def pick(stacked, layer):
    return lax.dynamic_index_in_dim(stacked[0], layer, 0, keepdims=False)


def body(activations, norm_gain, w_query, w_keyval, w_out, segment_ids, layer_order):
    ctx_count = lax.axis_size("ctx")
    ctx_index = lax.axis_index("ctx")
    state = activations[0]
    seqs_here, tok_rows, model_width = state.shape
    query_width = w_query.shape[-1]
    kv_width = w_keyval.shape[-1]
    head_dim = kv_width // 2
    in_rows = w_query.shape[2]
    wide = query_width + kv_width
    in_parts, out_parts = [], []
    for tick in range(TICKS):
        layer = layer_order[tick, 0]
        gain_rows = jnp.pad(pick(norm_gain, layer)[None, :], ((0, 15), (0, wide - in_rows)))
        both = jnp.concatenate([pick(w_query, layer), pick(w_keyval, layer)], axis=1)
        in_parts.append(jnp.concatenate([both, gain_rows], axis=0))
        out_parts.append(pick(w_out, layer))
    query_pos = row_positions(
        ctx_index * tok_rows + lax.iota(jnp.int32, tok_rows), tok_rows, ctx_count
    )
    query_seg = jnp.take(segment_ids, query_pos, axis=1)
    halves = segment_ids.reshape(seqs_here, 2, ctx_count, tok_rows // 2)
    by_row = jnp.stack([halves[:, 0], halves[:, 1, ::-1]], axis=2)
    key_seg = by_row.reshape(seqs_here, ctx_count * tok_rows)
    key_pos = row_positions(lax.iota(jnp.int32, ctx_count * tok_rows), tok_rows, ctx_count)
    allowed = (key_pos[None, None, :] <= query_pos[None, :, None]) & (
        key_seg[:, None, :] == query_seg[:, :, None]
    )
    bias = jnp.where(allowed[0], 0.0, -1e30)
    blocks = [part for pair in zip(in_parts, out_parts) for part in pair]
    state = run_layers(state[0], bias, blocks, ctx_count, head_dim)
    state = passed_along(state, "pipe", 1).astype(jnp.float32)[None]
    return state[None]


def solution(mesh):
    in_specs = (
        P("pipe", None, "ctx", None),
        P("pipe", None, "ctx"),
        P("pipe", None, "ctx", None),
        P("pipe", None, "ctx", None),
        P("pipe", None, None, "ctx"),
        P(),
        P(None, "pipe"),
    )
    out_specs = P("pipe", None, "ctx", None)
    return jax.shard_map(body, mesh=mesh, in_specs=in_specs, out_specs=out_specs, check_vma=False)
```

```python
import functools
import itertools
import math

import jax
import jax.numpy as jnp
from jax import lax
from jax.experimental import pallas as pl
from jax.experimental.pallas import tpu as pltpu
from jax.sharding import PartitionSpec as P

TICKS = 2


def passed_along(array, axis, by):
    length = lax.axis_size(axis)
    return lax.ppermute(array, axis, [(i, (i + by) % length) for i in range(length)])


def grid_of(count):
    known = {16: (4, 2, 2), 32: (4, 8)}
    return known.get(count, (count,))


def orders_of(sizes):
    dims = tuple(range(len(sizes)))
    if len(dims) == 1:
        return (dims, dims)
    return (dims, dims[:-2] + (dims[-1], dims[-2]))


def layers_kernel(sizes, cuts, *refs):
    weights = 2 * TICKS
    count = len(cuts)
    stream, bias = refs[0], refs[1]
    out = refs[2 + weights]
    scratch = refs[3 + weights :]
    blocks = refs[2 : 2 + weights] + scratch[:TICKS]
    wholes = scratch[TICKS : TICKS + count]
    queries, attended, leaving, arriving = scratch[TICKS + count : TICKS + count + 4]
    send_sems, recv_sems, own_sems, pipe_sems = scratch[TICKS + count + 4 :]
    rank = len(sizes)
    strides = [math.prod(sizes[d + 1 :]) for d in range(rank)]
    ctx_count = math.prod(sizes)
    me = lax.axis_index("ctx")
    coords = [(me // strides[d]) % sizes[d] for d in range(rank)]
    pipe_count = lax.axis_size("pipe")
    section = lax.axis_index("pipe")

    def place(delta):
        return sum(((coords[d] + delta[d]) % sizes[d]) * strides[d] for d in range(rank))

    def along(dim, by):
        return tuple(by if d == dim else 0 for d in range(rank))

    def flat(delta):
        return sum(delta[d] * strides[d] for d in range(rank))

    barrier = pltpu.get_barrier_semaphore()
    greeted = 0
    for dim in range(rank):
        for by in range(1, sizes[dim]):
            pl.semaphore_signal(
                barrier,
                inc=1,
                device_id={"ctx": place(along(dim, by))},
                device_id_type=pl.DeviceIdType.MESH,
            )
            greeted += 1
    for by in sorted({1, pipe_count - 1}):
        pl.semaphore_signal(
            barrier,
            inc=1,
            device_id={"pipe": (section + by) % pipe_count},
            device_id_type=pl.DeviceIdType.MESH,
        )
        greeted += 1
    pl.semaphore_wait(barrier, greeted)

    orders = orders_of(sizes)
    started = []
    used = {}

    def copy_of(which, part, delta, dim, by, send):
        rows = pl.ds(*cuts[which][part])
        landing = wholes[which].at[place(delta), rows]
        origin = landing if any(delta) else blocks[which].at[rows]
        seen = tuple((sizes[d] - by) % sizes[d] if d == dim else delta[d] for d in range(rank))
        return pltpu.make_async_remote_copy(
            src_ref=origin,
            dst_ref=landing,
            send_sem=send_sems.at[which, part, send],
            recv_sem=recv_sems.at[which, part, flat(seen)],
            device_id={"ctx": place(along(dim, by))},
            device_id_type=pl.DeviceIdType.MESH,
        )

    def pass_on(which, part, delta, phases):
        for phase in phases:
            dim = orders[part][phase]
            for by in range(1, sizes[dim]):
                send = used.get((which, part), 0)
                used[which, part] = send + 1
                copy = copy_of(which, part, delta, dim, by, send)
                copy.start()
                started.append(copy)

    def take(which, phase):
        for part, order in enumerate(orders):
            ranges = [range(1)] * rank
            for before in order[:phase]:
                ranges[before] = range(sizes[before])
            ranges[order[phase]] = range(1, sizes[order[phase]])
            for delta in itertools.product(*ranges):
                landing = wholes[which].at[place(delta), pl.ds(*cuts[which][part])]
                pltpu.make_async_remote_copy(
                    src_ref=landing,
                    dst_ref=landing,
                    send_sem=send_sems.at[which, part, 0],
                    recv_sem=recv_sems.at[which, part, flat(delta)],
                    device_id={"ctx": place(along(order[phase], 1))},
                    device_id_type=pl.DeviceIdType.MESH,
                ).wait_recv()
                pass_on(which, part, delta, range(phase + 1, rank))

    def own_copy(which):
        return pltpu.make_async_copy(blocks[which], wholes[which].at[me], own_sems.at[which])

    def begin(which):
        own_copy(which).start()
        for part in range(len(orders)):
            pass_on(which, part, (0,) * rank, range(rank))

    tok_rows, model_width = stream.shape
    in_rows = model_width // ctx_count
    query_width = attended.shape[1]
    head_dim = queries.shape[-1]
    head_count = query_width // head_dim
    scale = 1.0 / math.sqrt(head_dim)

    def columns(index):
        return pl.ds(pl.multiple_of(index * in_rows, in_rows), in_rows)

    def project(tick, source):
        own_copy(2 * tick).wait()
        whole = wholes[2 * tick]

        def square(index, total):
            value = source[:, columns(index)].astype(jnp.float32)
            return total + jnp.sum(value * value, axis=1, keepdims=True)

        squares = lax.fori_loop(0, ctx_count, square, jnp.zeros((tok_rows, 1), jnp.float32))
        factor = lax.rsqrt(squares / model_width + 1e-05)

        def piece(index, total):
            value = source[:, columns(index)].astype(jnp.float32)
            gain = wholes[0][index, in_rows : in_rows + 16, :in_rows].astype(jnp.float32)
            gain = gain[tick : tick + 1]
            hidden = (value * factor * gain).astype(jnp.bfloat16)
            return total + jnp.dot(
                hidden, whole[index, :in_rows, :], preferred_element_type=jnp.float32
            )

        width = whole.shape[-1]
        sums = lax.fori_loop(0, ctx_count, piece, jnp.zeros((tok_rows, width), jnp.float32))
        low = sums.astype(jnp.bfloat16)
        for head in range(head_count):
            queries[head] = low[:, head * head_dim : (head + 1) * head_dim]
        blocks[weights + tick][...] = low[:, query_width:]

    def attend(tick):
        own_copy(weights + tick).wait()
        whole = wholes[weights + tick]
        keys = whole[:, :, :head_dim].reshape(ctx_count * tok_rows, head_dim)
        values = whole[:, :, head_dim:].reshape(ctx_count * tok_rows, head_dim)
        for head in range(head_count):
            scores = lax.dot_general(
                queries[head], keys, (((1,), (1,)), ((), ())), preferred_element_type=jnp.float32
            )
            scores = scores * scale + bias[...]
            probs = jnp.exp(scores - jnp.max(scores, axis=1, keepdims=True))
            totals = jnp.sum(probs, axis=1, keepdims=True)
            summed = jnp.dot(
                probs.astype(jnp.bfloat16), values, preferred_element_type=jnp.float32
            )
            attended[:, head * head_dim : (head + 1) * head_dim] = (summed / totals).astype(
                jnp.bfloat16
            )

    def mix(tick, source, target):
        own_copy(2 * tick + 1).wait()
        whole = wholes[2 * tick + 1]

        @pl.loop(0, ctx_count)
        def _(index):
            mixed = jnp.dot(attended[...], whole[index], preferred_element_type=jnp.float32)
            value = source[:, columns(index)].astype(jnp.float32) + mixed
            target[:, columns(index)] = value.astype(jnp.bfloat16)

    last = rank - 1
    begin(0)
    begin(1)
    take(0, 0)
    begin(2)
    for phase in range(1, rank):
        take(0, phase)
        take(1, phase - 1)
    project(0, stream)
    begin(4)
    begin(3)
    for phase in range(rank):
        take(4, phase)
        if phase < last:
            take(2, phase)
    attend(0)
    for phase in range(last):
        take(3, phase)
    take(1, last)
    mix(0, stream, leaving)
    onward = pltpu.make_async_remote_copy(
        src_ref=leaving,
        dst_ref=arriving,
        send_sem=pipe_sems.at[0],
        recv_sem=pipe_sems.at[1],
        device_id={"pipe": (section + 1) % pipe_count},
        device_id_type=pl.DeviceIdType.MESH,
    )
    onward.start()
    take(2, last)
    onward.wait()
    project(1, arriving)
    begin(5)
    for phase in range(rank):
        take(5, phase)
    attend(1)
    take(3, last)
    mix(1, arriving, out)
    for copy in started:
        copy.wait_send()


def run_layers(stream, bias, blocks, ctx_count, head_dim):
    tok_rows = stream.shape[0]
    query_width = blocks[1].shape[0]
    kv_width = blocks[0].shape[1] - query_width
    shapes = [block.shape for block in blocks] + [(tok_rows, kv_width)] * TICKS
    cuts = []
    for rows, _ in shapes:
        first = rows // 32 * 16
        cuts.append(((0, first), (first, rows - first)))
    count = len(shapes)
    parts = len(cuts[0])
    low = jnp.bfloat16
    vmem = pl.BlockSpec(memory_space=pltpu.VMEM)
    return pl.pallas_call(
        functools.partial(layers_kernel, grid_of(ctx_count), tuple(cuts)),
        out_shape=jax.ShapeDtypeStruct(stream.shape, low),
        in_specs=[vmem, vmem] + [pl.BlockSpec(memory_space=pl.ANY)] * len(blocks),
        out_specs=vmem,
        scratch_shapes=[pltpu.VMEM((tok_rows, kv_width), low)] * TICKS
        + [pltpu.VMEM((ctx_count, *shape), low) for shape in shapes]
        + [
            pltpu.VMEM((query_width // head_dim, tok_rows, head_dim), low),
            pltpu.VMEM((tok_rows, query_width), low),
            pltpu.VMEM(stream.shape, low),
            pltpu.VMEM(stream.shape, low),
            pltpu.SemaphoreType.DMA((count, parts, ctx_count)),
            pltpu.SemaphoreType.DMA((count, parts, ctx_count)),
            pltpu.SemaphoreType.DMA((count,)),
            pltpu.SemaphoreType.DMA((2,)),
        ],
        compiler_params=pltpu.CompilerParams(
            collective_id=0, has_side_effects=True, vmem_limit_bytes=56 * 1024 * 1024
        ),
    )(stream, bias, *blocks)


def row_positions(rows, tok_rows, ctx_count):
    half = tok_rows // 2
    block = rows // tok_rows
    offset = rows % tok_rows
    return jnp.where(
        offset < half, block * half + offset, (2 * ctx_count - 1 - block) * half + offset - half
    )


def pick(stacked, layer):
    return lax.dynamic_index_in_dim(stacked[0], layer, 0, keepdims=False)


def body(activations, norm_gain, w_query, w_keyval, w_out, segment_ids, layer_order):
    ctx_count = lax.axis_size("ctx")
    ctx_index = lax.axis_index("ctx")
    state = activations[0]
    seqs_here, tok_rows, model_width = state.shape
    query_width = w_query.shape[-1]
    kv_width = w_keyval.shape[-1]
    head_dim = kv_width // 2
    in_rows = w_query.shape[2]
    wide = query_width + kv_width
    in_parts, out_parts = [], []
    for tick in range(TICKS):
        layer = layer_order[tick, 0]
        both = jnp.concatenate([pick(w_query, layer), pick(w_keyval, layer)], axis=1)
        if tick == 0:
            gains = jnp.stack([pick(norm_gain, layer_order[t, 0]) for t in range(TICKS)])
            gains = jnp.pad(gains, ((0, 16 - TICKS), (0, wide - in_rows)))
            both = jnp.concatenate([both, gains], axis=0)
        in_parts.append(both)
        out_parts.append(pick(w_out, layer))
    query_pos = row_positions(
        ctx_index * tok_rows + lax.iota(jnp.int32, tok_rows), tok_rows, ctx_count
    )
    halves = segment_ids.reshape(seqs_here, 2, ctx_count, tok_rows // 2)
    by_row = jnp.stack([halves[:, 0], halves[:, 1, ::-1]], axis=2)
    key_seg = by_row.reshape(seqs_here, ctx_count * tok_rows)
    query_seg = lax.dynamic_slice_in_dim(key_seg, ctx_index * tok_rows, tok_rows, axis=1)
    key_pos = row_positions(lax.iota(jnp.int32, ctx_count * tok_rows), tok_rows, ctx_count)
    allowed = (key_pos[None, None, :] <= query_pos[None, :, None]) & (
        key_seg[:, None, :] == query_seg[:, :, None]
    )
    bias = jnp.where(allowed[0], 0.0, -1e30)
    blocks = [part for pair in zip(in_parts, out_parts) for part in pair]
    state = run_layers(state[0], bias, blocks, ctx_count, head_dim)
    state = passed_along(state, "pipe", 1).astype(jnp.float32)[None]
    return state[None]


def solution(mesh):
    in_specs = (
        P("pipe", None, "ctx", None),
        P("pipe", None, "ctx"),
        P("pipe", None, "ctx", None),
        P("pipe", None, "ctx", None),
        P("pipe", None, None, "ctx"),
        P(),
        P(None, "pipe"),
    )
    out_specs = P("pipe", None, "ctx", None)
    return jax.shard_map(body, mesh=mesh, in_specs=in_specs, out_specs=out_specs, check_vma=False)
```
